128 devices in a mesh: row: 16 (over y, z), col: 8 (over x, core).
Axes of the slice: x: 4, y: 4, z: 4, core: 2. Of those that a mesh axis runs over, the one named last changes fastest.
Arguments:
- star_state: float32 [7, 262144], P(None, ('row', 'col')), as said below
- active_index: int32 [32768], P(('row', 'col')), may hold values from 0 to 2047, as said below
- neighbour_index: int32 [32768, 128], P(('row', 'col')), may hold values from 0 to 2047, as said below
- assignment: int32 [32768, 1], P(('row', 'col')), may hold values from 0 to 127, as said below
- start_state: float32 [6, 32768], P(None, ('row', 'col')), may hold values from -6 to 6
- old_derivs: float32 [6, 32768], P(None, ('row', 'col')), may hold values from -12 to 12
- step_size: float32 [32768], P(('row', 'col')), may hold values from 0.1 to 1
Outputs:
- corrected: float32 [6, 32768], P(None, ('row', 'col'))
- forces: float32 [12, 32768], P(None, ('row', 'col'))
The draws below stay inside these ranges and needn't reach their ends.
Inputs may be any that keep to these rules, and one draw needn't show every extreme that they name: `star_state`: row 6 (masses) is positive. `active_index`: within each aligned block of 256 entries (the active stars of one device) the entries are distinct. `neighbour_index`: the 128 entries of each row are distinct. `assignment`: within the rows of one device (aligned blocks of 256 rows) no device number appears more than 4 times, and some appears exactly 4 times.
All inputs are finite; a program needn't handle non-finite values.
Results may differ from the reference program's by a relative error of at most 0.000028.
Values sent between devices are 32-bit elements; how exact they have to be, the bound alone decides.
No kernel may reach another device: no remote copies, remote signals or barrier semaphores. Data moves between devices by JAX's collectives and lax.ppermute only.
A program may use at most 192 MiB of HBM per device.

```python
import math
import jax
import jax.numpy as jnp
from jax import lax

ACT_DEV = 256
S_DEV = 2048
K = 128
NACT = 32768
NSTARS = 262144
MOST = 4
DEVICES = 128


def pick_distinct(pick_key, count):
    order = jax.random.permutation(pick_key, S_DEV)
    return order[:count].astype(jnp.int32)


def pick_with_top(pick_key, count):
    order = jax.random.permutation(pick_key, S_DEV).astype(jnp.int32)
    places = jnp.arange(S_DEV, dtype=jnp.int32)
    swapped = jnp.where(order == S_DEV - 1, order[0], jnp.where(places == 0, S_DEV - 1, order))
    return swapped[:count].astype(jnp.int32)


def layout(seed_key):
    keys = jax.random.split(seed_key, 6)
    slots_total = DEVICES * MOST
    hot_count = max(1, ACT_DEV // (4 * MOST))
    hot_order = jax.random.permutation(keys[0], DEVICES).astype(jnp.int32)
    is_hot = (hot_order < hot_count).astype(jnp.int32)
    slot_owner = jnp.arange(slots_total, dtype=jnp.int32) // MOST
    slot_hot = is_hot[slot_owner]

    def one_block(block_key):
        split_keys = jax.random.split(block_key, 2)
        ranks = jax.random.permutation(split_keys[0], slots_total).astype(jnp.int32)
        scores = slot_hot * slots_total + ranks
        chosen = lax.top_k(scores, ACT_DEV)[1].astype(jnp.int32)
        targets = chosen // MOST
        return jax.random.permutation(split_keys[1], targets).astype(jnp.int32)
    targets = jax.vmap(one_block)(jax.random.split(keys[1], DEVICES)).reshape(NACT)
    actives = jax.vmap(lambda pick_key: pick_distinct(pick_key, ACT_DEV))(jax.random.split(keys[2], DEVICES))
    actives = actives.at[0].set(pick_with_top(keys[3], ACT_DEV)).reshape(NACT)
    neighbours = jax.vmap(lambda pick_key: pick_distinct(pick_key, K))(jax.random.split(keys[4], NACT))
    neighbours = neighbours.at[0].set(pick_with_top(keys[5], K))
    return (targets, actives, neighbours)


def draw_assignment(key, part):
    targets, actives, neighbours = layout(jax.random.fold_in(key, 11))
    return targets[:, None]


def draw_active_index(key, part):
    targets, actives, neighbours = layout(jax.random.fold_in(key, 11))
    return actives


def draw_neighbour_index(key, part):
    targets, actives, neighbours = layout(jax.random.fold_in(key, 11))
    return neighbours


def draw_star_state(key, part):
    targets, actives, neighbours = layout(jax.random.fold_in(key, 11))
    keys = jax.random.split(jax.random.fold_in(key, 12), 5)
    spread = 0.25
    velocity = 0.5 * jax.random.normal(keys[3], (3, NSTARS), jnp.float32)
    centers = 2.0 * jax.random.normal(keys[0], (3, DEVICES), jnp.float32)
    star_owner = jnp.arange(NSTARS, dtype=jnp.int32) // S_DEV
    place = centers[:, star_owner] + spread * jax.random.normal(keys[1], (3, NSTARS), jnp.float32)
    active_owner = jnp.arange(NACT, dtype=jnp.int32) // ACT_DEV
    global_index = (active_owner * S_DEV + actives).astype(jnp.int32)
    active_place = centers[:, targets] + spread * jax.random.normal(keys[2], (3, NACT), jnp.float32)
    place = place.at[:, global_index].set(active_place)
    log_mass = jax.random.uniform(keys[4], (1, NSTARS), jnp.float32, math.log(0.3), math.log(3.0))
    masses = jnp.exp(log_mass) * (0.1 / K)
    return jnp.concatenate([place, velocity, masses]).astype(jnp.float32)


def block_levels(own_key, extent, shards, least, largest):
    def one(dim, blocks):
        steps = jax.random.uniform(jax.random.fold_in(jax.random.fold_in(own_key, 6), dim), (blocks,), jnp.float32, least / len(shards), largest / len(shards))
        return jnp.repeat(jnp.exp(steps), extent[dim] // blocks).reshape((-1,) + (1,) * (len(extent) - dim - 1))

    loudness = one(*shards[0])
    for cut in shards[1:]:
        loudness = loudness * one(*cut)
    return loudness


def bell_draw(stream_key, dims, width, bound, shards=(), kind=jnp.bfloat16):
    entries = width * jax.random.normal(stream_key, dims, jnp.float32)
    if shards:
        entries = entries * block_levels(stream_key, dims, shards, -0.22, 0.18)
    return jnp.clip(entries, -bound, bound).astype(kind)


def setup_inputs(seed: int = 0) -> dict:
    seeds = jax.random.split(jax.random.key(seed), 8)
    return {
        "star_state": draw_star_state(jax.random.fold_in(seeds[7], 71), 0),
        "active_index": draw_active_index(jax.random.fold_in(seeds[7], 71), 0),
        "neighbour_index": draw_neighbour_index(jax.random.fold_in(seeds[7], 71), 0),
        "assignment": draw_assignment(jax.random.fold_in(seeds[7], 71), 0),
        "start_state": bell_draw(seeds[4], (6, NACT), 1.0, 6.0, ((1, 128),), jnp.float32),
        "old_derivs": bell_draw(seeds[5], (6, NACT), 2.0, 12.0, ((1, 128),), jnp.float32),
        "step_size": jnp.clip(jnp.exp(math.log(1.0) - 2.3025851 * jax.random.uniform(seeds[6], (NACT,), jnp.float32) ** block_levels(seeds[6], (NACT,), ((0, 128),), -0.2, 0.2)), 0.1, 1.0),
    }


soft_sq = 0.01

def pair_terms(active_parts, other_parts):
    sep_x = other_parts[0] - active_parts[0]
    sep_y = other_parts[1] - active_parts[1]
    sep_z = other_parts[2] - active_parts[2]
    rel_x = other_parts[3] - active_parts[3]
    rel_y = other_parts[4] - active_parts[4]
    rel_z = other_parts[5] - active_parts[5]
    dist_sq = sep_x * sep_x + sep_y * sep_y + sep_z * sep_z + soft_sq
    inverse = 1.0 / dist_sq
    strength = other_parts[6] * inverse * jnp.sqrt(inverse)
    radial = 3.0 * (sep_x * rel_x + sep_y * rel_y + sep_z * rel_z) * inverse
    pieces = [strength * sep_x, strength * sep_y, strength * sep_z, strength * (rel_x - radial * sep_x), strength * (rel_y - radial * sep_y), strength * (rel_z - radial * sep_z)]
    return jnp.stack([lax.optimization_barrier(jnp.sum(term, axis=-1)) for term in pieces])

def hermite(total, start_state, old_derivs, step_size):
    half_step = step_size * 0.5
    twelfth = step_size * step_size / 12.0
    old_acc, old_jerk = (old_derivs[:3], old_derivs[3:])
    new_acc, new_jerk = (total[:3], total[3:])
    old_pos, old_vel = (start_state[:3], start_state[3:])
    new_vel = old_vel + (old_acc + new_acc) * half_step + (old_jerk - new_jerk) * twelfth
    new_pos = old_pos + (old_vel + new_vel) * half_step + (old_acc - new_acc) * twelfth
    return jnp.concatenate([new_pos, new_vel])

def reference(star_state, active_index, neighbour_index, assignment, start_state, old_derivs, step_size):
    owner_dev = jnp.arange(NACT, dtype=jnp.int32) // ACT_DEV
    global_index = (owner_dev * S_DEV + active_index).astype(jnp.int32)
    active_state = jnp.take(star_state[:6], global_index, axis=1)
    block_len = math.gcd(NACT, 64)
    block_count = NACT // block_len
    blocks = active_state.reshape(6, block_count, block_len).transpose(1, 0, 2)
    star_rows = [star_state[component][None, :] for component in range(7)]

    def one_block(block_state):
        return pair_terms([block_state[component][:, None] for component in range(6)], star_rows)
    total = lax.map(one_block, blocks).transpose(1, 0, 2).reshape(6, NACT)
    neighbour_global = (assignment[:, 0][:, None] * S_DEV + neighbour_index).astype(jnp.int32)
    tile_data = jnp.take(star_state, neighbour_global, axis=1)
    irregular = pair_terms([active_state[component][:, None] for component in range(6)], [tile_data[component] for component in range(7)])
    regular = total - irregular
    corrected = hermite(total, start_state, old_derivs, step_size)
    return (corrected, jnp.concatenate([regular, irregular]))
```

```python
import functools

import jax
import jax.numpy as jnp
from jax import lax
from jax.experimental import pallas as pl
from jax.experimental.pallas import tpu as pltpu
from jax.sharding import PartitionSpec as P

F = jnp.float32
B = jnp.bfloat16
SOFT = 0.01
A = 256
K = 128
S = 2048
CH = 256


def pick_columns(table, low, high):
    out = jnp.zeros(low.shape, F)
    for g in range(S // 128):
        found = jnp.take_along_axis(table(g), low, axis=1, mode="promise_in_bounds")
        out = jnp.where(high == g, found, out)
    return out


def own_kernel(st_ref, idx_ref, q_ref, qc_ref, c_ref):
    for h in range(A // 128):
        idx = jnp.broadcast_to(idx_ref[0:1, h * 128 : (h + 1) * 128], (8, 128))
        pad = jnp.zeros((1, 128), F)
        table = lambda g: jnp.concatenate([st_ref[:, g * 128 : (g + 1) * 128], pad])
        q_ref[:, h * 128 : (h + 1) * 128] = pick_columns(table, idx & 127, idx >> 7)
    q = q_ref[...]
    row = lax.broadcasted_iota(jnp.int32, q.shape, 0)
    q = jnp.where(row < 6, q, 0.0)
    q_ref[...] = q
    wide = jnp.concatenate([q, jnp.zeros((120, A), F)])
    qc_ref[...] = wide.T
    c_ref[...] = jnp.broadcast_to(jnp.sum(q, axis=1, keepdims=True) * (1.0 / A), (8, 128))


def own_states(star_state, active_index):
    return pl.pallas_call(
        own_kernel,
        out_shape=(
            jax.ShapeDtypeStruct((8, A), F),
            jax.ShapeDtypeStruct((A, 128), F),
            jax.ShapeDtypeStruct((8, 128), F),
        ),
    )(star_state, active_index[None, :])


def pair_kernel(*refs, G, BB):
    NG=A//G
    pl.run_scoped(functools.partial(pair_body,*refs,G=G,BB=BB),*([pltpu.ACC(0)((G,256),F)]*NG+[pltpu.ACC(1)((G,256),F)]*NG))
def pair_body(_, st_ref, qc_ref, c_ref, o_ref, qb, wt, acc, *accs, G, BB):
    NG=A//G
    sacc=accs[:NG]; tacc=accs[NG:]
    TS=st_ref.shape[2]
    i=pl.program_id(0)
    @pl.when(i==0)
    def _():
        for c in range(6):
            qb[c]=jnp.broadcast_to(qc_ref[:,c:c+1],(A,128))
        acc[...]=jnp.zeros_like(acc)
    zw=jnp.zeros((256-32,CH),B)
    for b in range(BB):
        s=jnp.concatenate([st_ref[b],jnp.zeros((1,TS),F)],axis=0)
        row=lax.broadcasted_iota(jnp.int32,s.shape,0)
        w=(s-c_ref[:,0:1])*jnp.where(row<6,s[6:7],1.0)
        p=[]
        for _ in range(3):
            h=w.astype(B).astype(F); p.append(h); w=w-h
        wt[...]=jnp.concatenate(p+[jnp.zeros((8,TS),F)],axis=0).astype(B)
        def chunk(k,_):
            cs=pl.ds(pl.multiple_of(k*CH,CH),CH)
            ww=jnp.concatenate([wt[:,cs],zw],axis=0)
            for mx in range(2): pltpu.matmul_push_rhs(ww,0,mx,transpose=True)
            st=[jnp.broadcast_to(st_ref[b,r:r+1,cs],(G,CH)) for r in range(6)]
            for g in range(NG):
                rs=slice(g*G,(g+1)*G)
                q=[jnp.concatenate([qb[c,rs,:]]*2,axis=1) for c in range(6)]
                dx,dy,dz,wx,wy,wz=[st[c]-q[c] for c in range(6)]
                s2=(dx*dx+dy*dy)+(dz*dz+0.01)
                dw=(dx*wx+dy*wy)+dz*wz
                r=lax.rsqrt(s2); r2=r*r; S=r2*r; T=S*(r2*dw)
                sh=S.astype(B); sl=(S-sh.astype(F)).astype(B)
                th=T.astype(B); tl=(T-th.astype(F)).astype(B)
                ld=0 if g==0 else None
                pltpu.matmul_acc_lhs(sacc[g],sh,load_staged_rhs=ld)
                pltpu.matmul_acc_lhs(tacc[g],th,load_staged_rhs=ld)
                pltpu.matmul_acc_lhs(sacc[g],sl)
                pltpu.matmul_acc_lhs(tacc[g],tl)
            return 0
        lax.fori_loop(0,TS//CH,chunk,0)
    for g in range(NG):
        rs=slice(g*G,(g+1)*G)
        acc[0,rs,:]+=pltpu.matmul_pop(sacc[g])[:,:128]
        acc[1,rs,:]+=pltpu.matmul_pop(tacc[g])[:,:128]
    @pl.when(i==pl.num_programs(0)-1)
    def _():
        for c in range(2): o_ref[c]=acc[c].T[0:32]
def pair_sums(offset, blocks, st, qc, c, G=16, BB=4):
    D, _, TS = st.shape
    steps = D // BB
    return pl.pallas_call(
        functools.partial(pair_kernel, G=G, BB=BB),
        grid_spec=pltpu.PrefetchScalarGridSpec(
            num_scalar_prefetch=1,
            grid=(blocks // BB,),
            in_specs=[
                pl.BlockSpec((BB, 7, TS), lambda i, o: (lax.rem(i + o[0], steps), 0, 0)),
                pl.BlockSpec((A, 128), lambda i, o: (0, 0)),
                pl.BlockSpec((8, 128), lambda i, o: (0, 0)),
            ],
            out_specs=pl.BlockSpec((2, 32, A), lambda i, o: (0, 0, 0)),
            scratch_shapes=[
                pltpu.VMEM((6, A, 128), F),
                pltpu.VMEM((32, TS), B),
                pltpu.VMEM((2, A, 128), F),
            ],
        ),
        out_shape=jax.ShapeDtypeStruct((2, 32, A), F),
        compiler_params=pltpu.CompilerParams(vmem_limit_bytes=40 << 20),
        cost_estimate=pl.CostEstimate(
            flops=40 * A * S * blocks, bytes_accessed=32 * S * blocks, transcendentals=A * S * blocks
        ),
    )(offset, st, qc, c)


def final_kernel(
    as_ref, st_ref, nb_ref, qc_ref, q_ref, c_ref, s1_ref, s2_ref, start_ref, old_ref, h_ref, cor_ref, for_ref, near
):
    pad = jnp.zeros((1, 128), F)

    def gather(t, _):
        a = t * 4
        for u in range(4):
            dev = as_ref[a + u]
            idx = jnp.broadcast_to(nb_ref[pl.ds(a + u, 1), :], (8, 128))
            table = lambda g: jnp.concatenate([st_ref[dev, :, g * 128 : (g + 1) * 128], pad])
            near[a + u] = pick_columns(table, idx & 127, idx >> 7)
        return 0

    lax.fori_loop(0, A // 4, gather, 0)
    d = [near[:, r, :] - qc_ref[:, r : r + 1] for r in range(6)]
    dx, dy, dz, wx, wy, wz = d
    dist = dx * dx + dy * dy + dz * dz + SOFT
    inv = 1.0 / dist
    strength = near[:, 6, :] * inv * jnp.sqrt(inv)
    radial = 3.0 * (dx * wx + dy * wy + dz * wz) * inv
    cols = [
        jnp.sum(x, axis=1, keepdims=True)
        for x in (
            strength * dx,
            strength * dy,
            strength * dz,
            strength * (wx - radial * dx),
            strength * (wy - radial * dy),
            strength * (wz - radial * dz),
        )
    ]
    irregular = jnp.concatenate(cols + [jnp.zeros((A, 122), F)], axis=1).T[0:6]
    p = s1_ref[...] + s2_ref[...]
    p = (p[:, 16:24] + p[:, 8:16]) + p[:, 0:8]
    q = q_ref[...] - c_ref[:, 0:1]
    ps, pt = p[0], p[1]
    acc = ps[0:3] - q[0:3] * ps[6:7]
    jerk = (ps[3:6] - q[3:6] * ps[6:7]) - 3.0 * (pt[0:3] - q[0:3] * pt[6:7])
    total = jnp.concatenate([acc, jerk])
    for_ref[...] = jnp.concatenate([total - irregular, irregular])
    h = h_ref[...]
    half = h * 0.5
    twelfth = h * h / 12.0
    a0, j0 = old_ref[0:3, :], old_ref[3:6, :]
    x0, v0 = start_ref[0:3, :], start_ref[3:6, :]
    v1 = v0 + (a0 + acc) * half + (j0 - jerk) * twelfth
    x1 = x0 + (v0 + v1) * half + (a0 - acc) * twelfth
    cor_ref[...] = jnp.concatenate([x1, v1])


def finish(assignment, st, neighbours, qc, q, c, s1, s2, start, old, step):
    whole = pl.BlockSpec(memory_space=pltpu.VMEM)
    return pl.pallas_call(
        final_kernel,
        in_specs=[pl.BlockSpec(memory_space=pltpu.SMEM)] + [whole] * 10,
        out_specs=(whole, whole),
        out_shape=(jax.ShapeDtypeStruct((6, A), F), jax.ShapeDtypeStruct((12, A), F)),
        scratch_shapes=[pltpu.VMEM((A, 8, 128), F)],
        compiler_params=pltpu.CompilerParams(vmem_limit_bytes=40 << 20),
    )(assignment[:, 0], st, neighbours, qc, q, c, s1, s2, start, old, step[None, :])


def body(star_state, active_index, neighbour_index, assignment, start_state, old_derivs, step_size):
    rows, cols = lax.axis_size("row"), lax.axis_size("col")
    group = lax.all_gather(star_state, "col")
    every = lax.all_gather(group, "row").reshape(rows * cols, 7, S)
    q, qc, c = own_states(star_state, active_index)
    zero = jnp.zeros((1,), jnp.int32)
    near = pair_sums(zero, cols, group, qc, c)
    skip = ((lax.axis_index("row") + 1) * (cols // 4)).astype(jnp.int32).reshape(1)
    far = pair_sums(skip, (rows - 1) * cols, every, qc, c)
    return finish(assignment, every, neighbour_index, qc, q, c, near, far, start_state, old_derivs, step_size)


def solution(mesh):
    both = ("row", "col")
    in_specs = (P(None, both), P(both), P(both, None), P(both, None), P(None, both), P(None, both), P(both))
    out_specs = (P(None, both), P(None, both))
    return jax.shard_map(body, mesh=mesh, in_specs=in_specs, out_specs=out_specs, check_vma=False)
```

```python
import functools

import jax
import jax.numpy as jnp
from jax import lax
from jax.experimental import pallas as pl
from jax.experimental.pallas import tpu as pltpu
from jax.sharding import PartitionSpec as P

F = jnp.float32
B = jnp.bfloat16
SOFT = 0.01
A = 256
K = 128
S = 2048
CH = 256


def pick_columns(table, low, high):
    out = jnp.zeros(low.shape, F)
    for g in range(S // 128):
        found = jnp.take_along_axis(table(g), low, axis=1, mode="promise_in_bounds")
        out = jnp.where(high == g, found, out)
    return out


def own_kernel(st_ref, idx_ref, q_ref, qc_ref, c_ref):
    for h in range(A // 128):
        idx = jnp.broadcast_to(idx_ref[0:1, h * 128 : (h + 1) * 128], (8, 128))
        table = lambda g: st_ref[:, g * 128 : (g + 1) * 128]
        q_ref[:, h * 128 : (h + 1) * 128] = pick_columns(table, idx & 127, idx >> 7)
    q = q_ref[...]
    row = lax.broadcasted_iota(jnp.int32, q.shape, 0)
    q = jnp.where(row < 6, q, 0.0)
    q_ref[...] = q
    wide = jnp.concatenate([q, jnp.zeros((120, A), F)])
    qc_ref[...] = wide.T
    c_ref[...] = jnp.broadcast_to(jnp.sum(q, axis=1, keepdims=True) * (1.0 / A), (8, 128))


def own_states(stars, active_index):
    return pl.pallas_call(
        own_kernel,
        out_shape=(
            jax.ShapeDtypeStruct((8, A), F),
            jax.ShapeDtypeStruct((A, 128), F),
            jax.ShapeDtypeStruct((8, 128), F),
        ),
    )(stars, active_index[None, :])


def pair_kernel(*refs, G, BB):
    NG=A//G
    pl.run_scoped(functools.partial(pair_body,*refs,G=G,BB=BB),*([pltpu.ACC(0)((G,256),F)]*NG+[pltpu.ACC(1)((G,256),F)]*NG))
def pair_body(_, st_ref, qc_ref, c_ref, o_ref, qb, wt, acc, *accs, G, BB):
    NG=A//G
    sacc=accs[:NG]; tacc=accs[NG:]
    TS=st_ref.shape[3]
    i=pl.program_id(0)
    @pl.when(i==0)
    def _():
        for c in range(6):
            qb[c]=jnp.broadcast_to(qc_ref[:,c:c+1],(A,128))
        acc[...]=jnp.zeros_like(acc)
    zw=jnp.zeros((256-32,CH),B)
    def block(b, _):
        s=st_ref[0,b]
        row=lax.broadcasted_iota(jnp.int32,s.shape,0)
        w=(s-c_ref[:,0:1])*jnp.where(row<6,s[6:7],1.0)
        p=[]
        for _ in range(3):
            h=w.astype(B).astype(F); p.append(h); w=w-h
        wt[...]=jnp.concatenate(p+[jnp.zeros((8,TS),F)],axis=0).astype(B)
        def chunk(k,_):
            cs=pl.ds(pl.multiple_of(k*CH,CH),CH)
            ww=jnp.concatenate([wt[:,cs],zw],axis=0)
            for mx in range(2): pltpu.matmul_push_rhs(ww,0,mx,transpose=True)
            st=[jnp.broadcast_to(st_ref[0,b,r:r+1,cs],(G,CH)) for r in range(6)]
            for g in range(NG):
                rs=slice(g*G,(g+1)*G)
                q=[jnp.concatenate([qb[c,rs,:]]*2,axis=1) for c in range(6)]
                dx,dy,dz,wx,wy,wz=[st[c]-q[c] for c in range(6)]
                s2=(dx*dx+dy*dy)+(dz*dz+0.01)
                dw=(dx*wx+dy*wy)+dz*wz
                r=lax.rsqrt(s2); r2=r*r; S=r2*r; T=S*(r2*dw)
                sh=S.astype(B); sl=(S-sh.astype(F)).astype(B)
                th=T.astype(B); tl=(T-th.astype(F)).astype(B)
                ld=0 if g==0 else None
                pltpu.matmul_acc_lhs(sacc[g],sh,load_staged_rhs=ld)
                pltpu.matmul_acc_lhs(tacc[g],th,load_staged_rhs=ld)
                pltpu.matmul_acc_lhs(sacc[g],sl)
                pltpu.matmul_acc_lhs(tacc[g],tl)
            return 0
        lax.fori_loop(0,TS//CH,chunk,0)
        return 0
    lax.fori_loop(0,BB,block,0)
    for g in range(NG):
        rs=slice(g*G,(g+1)*G)
        acc[0,rs,:]+=pltpu.matmul_pop(sacc[g])[:,:128]
        acc[1,rs,:]+=pltpu.matmul_pop(tacc[g])[:,:128]
    @pl.when(i==pl.num_programs(0)-1)
    def _():
        for c in range(2): o_ref[c]=acc[c].T[0:32]
def pair_sums(first, ranks, st, qc, c, G=16):
    R, BB, _, TS = st.shape
    pairs = A * ranks * BB * TS
    return pl.pallas_call(
        functools.partial(pair_kernel, G=G, BB=BB),
        grid_spec=pltpu.PrefetchScalarGridSpec(
            num_scalar_prefetch=1,
            grid=(ranks,),
            in_specs=[
                pl.BlockSpec((1, BB, 8, TS), lambda i, o: (lax.rem(i + o[0], R), 0, 0, 0)),
                pl.BlockSpec((A, 128), lambda i, o: (0, 0)),
                pl.BlockSpec((8, 128), lambda i, o: (0, 0)),
            ],
            out_specs=pl.BlockSpec((2, 32, A), lambda i, o: (0, 0, 0)),
            scratch_shapes=[
                pltpu.VMEM((6, A, 128), F),
                pltpu.VMEM((32, TS), B),
                pltpu.VMEM((2, A, 128), F),
            ],
        ),
        out_shape=jax.ShapeDtypeStruct((2, 32, A), F),
        compiler_params=pltpu.CompilerParams(vmem_limit_bytes=40 << 20),
        cost_estimate=pl.CostEstimate(
            flops=40 * pairs, bytes_accessed=32 * ranks * BB * TS, transcendentals=pairs
        ),
    )(first, st, qc, c)


def final_kernel(
    as_ref, sa_ref, sb_ref, nb_ref, qc_ref, q_ref, c_ref, s1_ref, s2_ref, s3_ref, start_ref, old_ref, h_ref, cor_ref, for_ref, near
):
    split = sa_ref.shape[3] // 128

    def lanes(dev, g):
        row, col = lax.div(dev, sa_ref.shape[1]), lax.rem(dev, sa_ref.shape[1])
        ref, h = (sa_ref, g) if g < split else (sb_ref, g - split)
        return ref[row, col, :, h * 128 : (h + 1) * 128]

    def gather(t, _):
        a = t * 4
        for u in range(4):
            dev = as_ref[a + u]
            idx = jnp.broadcast_to(nb_ref[pl.ds(a + u, 1), :], (8, 128))
            near[a + u] = pick_columns(functools.partial(lanes, dev), idx & 127, idx >> 7)
        return 0

    lax.fori_loop(0, A // 4, gather, 0)
    d = [near[:, r, :] - qc_ref[:, r : r + 1] for r in range(6)]
    dx, dy, dz, wx, wy, wz = d
    dist = dx * dx + dy * dy + dz * dz + SOFT
    inv = 1.0 / dist
    strength = near[:, 6, :] * inv * jnp.sqrt(inv)
    radial = 3.0 * (dx * wx + dy * wy + dz * wz) * inv
    cols = [
        jnp.sum(x, axis=1, keepdims=True)
        for x in (
            strength * dx,
            strength * dy,
            strength * dz,
            strength * (wx - radial * dx),
            strength * (wy - radial * dy),
            strength * (wz - radial * dz),
        )
    ]
    irregular = jnp.concatenate(cols + [jnp.zeros((A, 122), F)], axis=1).T[0:6]
    p = (s1_ref[...] + s2_ref[...]) + s3_ref[...]
    p = (p[:, 16:24] + p[:, 8:16]) + p[:, 0:8]
    q = q_ref[...] - c_ref[:, 0:1]
    ps, pt = p[0], p[1]
    acc = ps[0:3] - q[0:3] * ps[6:7]
    jerk = (ps[3:6] - q[3:6] * ps[6:7]) - 3.0 * (pt[0:3] - q[0:3] * pt[6:7])
    total = jnp.concatenate([acc, jerk])
    for_ref[...] = jnp.concatenate([total - irregular, irregular])
    h = h_ref[...]
    half = h * 0.5
    twelfth = h * h / 12.0
    a0, j0 = old_ref[0:3, :], old_ref[3:6, :]
    x0, v0 = start_ref[0:3, :], start_ref[3:6, :]
    v1 = v0 + (a0 + acc) * half + (j0 - jerk) * twelfth
    x1 = x0 + (v0 + v1) * half + (a0 - acc) * twelfth
    cor_ref[...] = jnp.concatenate([x1, v1])


def finish(assignment, sa, sb, neighbours, qc, q, c, s1, s2, s3, start, old, step):
    whole = pl.BlockSpec(memory_space=pltpu.VMEM)
    return pl.pallas_call(
        final_kernel,
        in_specs=[pl.BlockSpec(memory_space=pltpu.SMEM)] + [whole] * 12,
        out_specs=(whole, whole),
        out_shape=(jax.ShapeDtypeStruct((6, A), F), jax.ShapeDtypeStruct((12, A), F)),
        scratch_shapes=[pltpu.VMEM((A, 8, 128), F)],
        compiler_params=pltpu.CompilerParams(vmem_limit_bytes=40 << 20),
    )(assignment[:, 0], sa, sb, neighbours, qc, q, c, s1, s2, s3, start, old, step[None, :])


def body(star_state, active_index, neighbour_index, assignment, start_state, old_derivs, step_size):
    rows = lax.axis_size("row")
    cut = S // 4
    stars = jnp.pad(star_state, ((0, 1), (0, 0)))
    group = lax.all_gather(stars, "col")
    part_a = lax.all_gather(group[:, :, :cut], "row")
    part_b = lax.all_gather(group[:, :, cut:], "row")
    q, qc, c = own_states(stars, active_index)
    zero = jnp.zeros((1,), jnp.int32)
    after = (lax.axis_index("row") + 1).astype(jnp.int32).reshape(1)
    near = pair_sums(zero, 1, group[None], qc, c)
    far_a = pair_sums(after, rows - 1, part_a, qc, c)
    far_b = pair_sums(after, rows - 1, part_b, qc, c)
    return finish(
        assignment, part_a, part_b, neighbour_index, qc, q, c, near, far_a, far_b, start_state, old_derivs, step_size
    )


def solution(mesh):
    both = ("row", "col")
    in_specs = (P(None, both), P(both), P(both, None), P(both, None), P(None, both), P(None, both), P(both))
    out_specs = (P(None, both), P(None, both))
    return jax.shard_map(body, mesh=mesh, in_specs=in_specs, out_specs=out_specs, check_vma=False)
```

```python
import functools

import jax
import jax.numpy as jnp
from jax import lax
from jax.experimental import pallas as pl
from jax.experimental.pallas import tpu as pltpu
from jax.sharding import PartitionSpec as P

F = jnp.float32
B = jnp.bfloat16
SOFT = 0.01
A = 256
K = 128
S = 2048
CH = 256
AHEAD = 3


def pick_columns(table, low, high):
    out = jnp.zeros(low.shape, F)
    for g in range(S // 128):
        found = jnp.take_along_axis(table(g), low, axis=1, mode="promise_in_bounds")
        out = jnp.where(high == g, found, out)
    return out


def own_kernel(st_ref, idx_ref, q_ref, qc_ref, c_ref):
    for h in range(A // 128):
        idx = jnp.broadcast_to(idx_ref[0:1, h * 128 : (h + 1) * 128], (8, 128))
        table = lambda g: st_ref[:, g * 128 : (g + 1) * 128]
        q_ref[:, h * 128 : (h + 1) * 128] = pick_columns(table, idx & 127, idx >> 7)
    q = q_ref[...]
    row = lax.broadcasted_iota(jnp.int32, q.shape, 0)
    q = jnp.where(row < 6, q, 0.0)
    q_ref[...] = q
    wide = jnp.concatenate([q, jnp.zeros((120, A), F)])
    qc_ref[...] = wide.T
    c_ref[...] = jnp.broadcast_to(jnp.sum(q, axis=1, keepdims=True) * (1.0 / A), (8, 128))


def own_states(stars, active_index):
    return pl.pallas_call(
        own_kernel,
        out_shape=(
            jax.ShapeDtypeStruct((8, A), F),
            jax.ShapeDtypeStruct((A, 128), F),
            jax.ShapeDtypeStruct((8, 128), F),
        ),
    )(stars, active_index[None, :])


def pair_kernel(*refs, G, BB):
    NG=A//G
    pl.run_scoped(functools.partial(pair_body,*refs,G=G,BB=BB),*([pltpu.ACC(0)((G,256),F)]*NG+[pltpu.ACC(1)((G,256),F)]*NG))
def pair_body(_, st_ref, qc_ref, c_ref, o_ref, qb, wt, acc, *accs, G, BB):
    NG=A//G
    sacc=accs[:NG]; tacc=accs[NG:]
    TS=st_ref.shape[3]
    i=pl.program_id(0)
    @pl.when(i==0)
    def _():
        for c in range(6):
            qb[c]=jnp.broadcast_to(qc_ref[:,c:c+1],(A,128))
        acc[...]=jnp.zeros_like(acc)
    zw=jnp.zeros((256-32,CH),B)
    def block(b, _):
        s=st_ref[0,b]
        row=lax.broadcasted_iota(jnp.int32,s.shape,0)
        w=(s-c_ref[:,0:1])*jnp.where(row<6,s[6:7],1.0)
        p=[]
        for _ in range(3):
            h=w.astype(B).astype(F); p.append(h); w=w-h
        wt[...]=jnp.concatenate(p+[jnp.zeros((8,TS),F)],axis=0).astype(B)
        def chunk(k,_):
            cs=pl.ds(pl.multiple_of(k*CH,CH),CH)
            ww=jnp.concatenate([wt[:,cs],zw],axis=0)
            for mx in range(2): pltpu.matmul_push_rhs(ww,0,mx,transpose=True)
            st=[jnp.broadcast_to(st_ref[0,b,r:r+1,cs],(G,CH)) for r in range(6)]
            for g in range(NG):
                rs=slice(g*G,(g+1)*G)
                q=[jnp.concatenate([qb[c,rs,:]]*2,axis=1) for c in range(6)]
                dx,dy,dz,wx,wy,wz=[st[c]-q[c] for c in range(6)]
                s2=(dx*dx+dy*dy)+(dz*dz+0.01)
                dw=(dx*wx+dy*wy)+dz*wz
                r=lax.rsqrt(s2); r2=r*r; S=r2*r; T=S*(r2*dw)
                sh=S.astype(B); sl=(S-sh.astype(F)).astype(B)
                th=T.astype(B); tl=(T-th.astype(F)).astype(B)
                ld=0 if g==0 else None
                pltpu.matmul_acc_lhs(sacc[g],sh,load_staged_rhs=ld)
                pltpu.matmul_acc_lhs(tacc[g],th,load_staged_rhs=ld)
                pltpu.matmul_acc_lhs(sacc[g],sl)
                pltpu.matmul_acc_lhs(tacc[g],tl)
            return 0
        lax.fori_loop(0,TS//CH,chunk,0)
        return 0
    lax.fori_loop(0,BB,block,0)
    for g in range(NG):
        rs=slice(g*G,(g+1)*G)
        acc[0,rs,:]+=pltpu.matmul_pop(sacc[g])[:,:128]
        acc[1,rs,:]+=pltpu.matmul_pop(tacc[g])[:,:128]
    @pl.when(i==pl.num_programs(0)-1)
    def _():
        for c in range(2): o_ref[c]=acc[c].T[0:32]
def pair_sums(first, ranks, st, qc, c, G=16):
    R, BB, _, TS = st.shape
    pairs = A * ranks * BB * TS
    return pl.pallas_call(
        functools.partial(pair_kernel, G=G, BB=BB),
        grid_spec=pltpu.PrefetchScalarGridSpec(
            num_scalar_prefetch=1,
            grid=(ranks,),
            in_specs=[
                pl.BlockSpec((1, BB, 8, TS), lambda i, o: (lax.rem(i + o[0], R), 0, 0, 0)),
                pl.BlockSpec((A, 128), lambda i, o: (0, 0)),
                pl.BlockSpec((8, 128), lambda i, o: (0, 0)),
            ],
            out_specs=pl.BlockSpec((2, 32, A), lambda i, o: (0, 0, 0)),
            scratch_shapes=[
                pltpu.VMEM((6, A, 128), F),
                pltpu.VMEM((32, TS), B),
                pltpu.VMEM((2, A, 128), F),
            ],
        ),
        out_shape=jax.ShapeDtypeStruct((2, 32, A), F),
        compiler_params=pltpu.CompilerParams(vmem_limit_bytes=40 << 20),
        cost_estimate=pl.CostEstimate(
            flops=40 * pairs, bytes_accessed=32 * ranks * BB * TS, transcendentals=pairs
        ),
    )(first, st, qc, c)


def final_kernel(
    as_ref, st_ref, nb_ref, qc_ref, q_ref, c_ref, *rest
):
    *sums, start_ref, old_ref, h_ref, cor_ref, for_ref, near = rest

    def lanes(dev, g):
        row, col = lax.div(dev, st_ref.shape[1]), lax.rem(dev, st_ref.shape[1])
        return st_ref[row, col, :, g * 128 : (g + 1) * 128]

    def gather(t, _):
        a = t * 4
        for u in range(4):
            dev = as_ref[a + u]
            idx = jnp.broadcast_to(nb_ref[pl.ds(a + u, 1), :], (8, 128))
            near[a + u] = pick_columns(functools.partial(lanes, dev), idx & 127, idx >> 7)
        return 0

    lax.fori_loop(0, A // 4, gather, 0)
    d = [near[:, r, :] - qc_ref[:, r : r + 1] for r in range(6)]
    dx, dy, dz, wx, wy, wz = d
    dist = dx * dx + dy * dy + dz * dz + SOFT
    inv = 1.0 / dist
    strength = near[:, 6, :] * inv * jnp.sqrt(inv)
    radial = 3.0 * (dx * wx + dy * wy + dz * wz) * inv
    cols = [
        jnp.sum(x, axis=1, keepdims=True)
        for x in (
            strength * dx,
            strength * dy,
            strength * dz,
            strength * (wx - radial * dx),
            strength * (wy - radial * dy),
            strength * (wz - radial * dz),
        )
    ]
    irregular = jnp.concatenate(cols + [jnp.zeros((A, 122), F)], axis=1).T[0:6]
    p = sum(ref[...] for ref in sums[1:]) + sums[0][...]
    p = (p[:, 16:24] + p[:, 8:16]) + p[:, 0:8]
    q = q_ref[...] - c_ref[:, 0:1]
    ps, pt = p[0], p[1]
    acc = ps[0:3] - q[0:3] * ps[6:7]
    jerk = (ps[3:6] - q[3:6] * ps[6:7]) - 3.0 * (pt[0:3] - q[0:3] * pt[6:7])
    total = jnp.concatenate([acc, jerk])
    for_ref[...] = jnp.concatenate([total - irregular, irregular])
    h = h_ref[...]
    half = h * 0.5
    twelfth = h * h / 12.0
    a0, j0 = old_ref[0:3, :], old_ref[3:6, :]
    x0, v0 = start_ref[0:3, :], start_ref[3:6, :]
    v1 = v0 + (a0 + acc) * half + (j0 - jerk) * twelfth
    x1 = x0 + (v0 + v1) * half + (a0 - acc) * twelfth
    cor_ref[...] = jnp.concatenate([x1, v1])


def finish(assignment, st, neighbours, qc, q, c, sums, start, old, step):
    whole = pl.BlockSpec(memory_space=pltpu.VMEM)
    return pl.pallas_call(
        final_kernel,
        in_specs=[pl.BlockSpec(memory_space=pltpu.SMEM)] + [whole] * (8 + len(sums)),
        out_specs=(whole, whole),
        out_shape=(jax.ShapeDtypeStruct((6, A), F), jax.ShapeDtypeStruct((12, A), F)),
        scratch_shapes=[pltpu.VMEM((A, 8, 128), F)],
        compiler_params=pltpu.CompilerParams(vmem_limit_bytes=40 << 20),
    )(assignment[:, 0], st, neighbours, qc, q, c, *sums, start, old, step[None, :])


def body(star_state, active_index, neighbour_index, assignment, start_state, old_derivs, step_size):
    rows = lax.axis_size("row")
    stars = jnp.pad(star_state, ((0, 1), (0, 0)))
    group = lax.all_gather(stars, "col")
    ahead = [
        lax.ppermute(group, "row", [((r + step) % rows, r) for r in range(rows)]) for step in range(1, AHEAD + 1)
    ]
    every = lax.all_gather(group, "row")
    q, qc, c = own_states(stars, active_index)
    zero = jnp.zeros((1,), jnp.int32)
    after = (lax.axis_index("row") + 1 + AHEAD).astype(jnp.int32).reshape(1)
    sums = [pair_sums(zero, 1, g[None], qc, c) for g in [group, *ahead]]
    sums.append(pair_sums(after, rows - 1 - AHEAD, every, qc, c))
    return finish(assignment, every, neighbour_index, qc, q, c, sums, start_state, old_derivs, step_size)


def solution(mesh):
    both = ("row", "col")
    in_specs = (P(None, both), P(both), P(both, None), P(both, None), P(None, both), P(None, both), P(both))
    out_specs = (P(None, both), P(None, both))
    return jax.shard_map(body, mesh=mesh, in_specs=in_specs, out_specs=out_specs, check_vma=False)
```

```python
import functools

import jax
import jax.numpy as jnp
from jax import lax
from jax.experimental import pallas as pl
from jax.experimental.pallas import tpu as pltpu
from jax.sharding import PartitionSpec as P

F = jnp.float32
B = jnp.bfloat16
SOFT = 0.01
A = 256
K = 128
S = 2048
CH = 256
AHEAD = 3


def pick_columns(table, low, high):
    out = jnp.zeros(low.shape, F)
    for g in range(S // 128):
        found = jnp.take_along_axis(table(g), low, axis=1, mode="promise_in_bounds")
        out = jnp.where(high == g, found, out)
    return out


def own_kernel(st_ref, idx_ref, q_ref, qc_ref, c_ref):
    for h in range(A // 128):
        idx = jnp.broadcast_to(idx_ref[0:1, h * 128 : (h + 1) * 128], (8, 128))
        table = lambda g: st_ref[:, g * 128 : (g + 1) * 128]
        q_ref[:, h * 128 : (h + 1) * 128] = pick_columns(table, idx & 127, idx >> 7)
    q = q_ref[...]
    row = lax.broadcasted_iota(jnp.int32, q.shape, 0)
    q = jnp.where(row < 6, q, 0.0)
    q_ref[...] = q
    wide = jnp.concatenate([q, jnp.zeros((120, A), F)])
    qc_ref[...] = wide.T
    c_ref[...] = jnp.broadcast_to(jnp.sum(q, axis=1, keepdims=True) * (1.0 / A), (8, 128))


def own_states(stars, active_index):
    return pl.pallas_call(
        own_kernel,
        out_shape=(
            jax.ShapeDtypeStruct((8, A), F),
            jax.ShapeDtypeStruct((A, 128), F),
            jax.ShapeDtypeStruct((8, 128), F),
        ),
    )(stars, active_index[None, :])


def pair_kernel(*refs, G, BB):
    NG=A//G
    pl.run_scoped(functools.partial(pair_body,*refs,G=G,BB=BB),*([pltpu.ACC(0)((G,256),F)]*NG+[pltpu.ACC(1)((G,256),F)]*NG))
def pair_body(_, st_ref, qc_ref, c_ref, o_ref, qb, wt, acc, *accs, G, BB):
    NG=A//G
    sacc=accs[:NG]; tacc=accs[NG:]
    TS=st_ref.shape[3]
    i=pl.program_id(0)
    @pl.when(i==0)
    def _():
        for c in range(6):
            qb[c]=jnp.broadcast_to(qc_ref[:,c:c+1],(A,128))
        acc[...]=jnp.zeros_like(acc)
    zw=jnp.zeros((256-32,CH),B)
    def block(b, _):
        s=st_ref[0,b]
        row=lax.broadcasted_iota(jnp.int32,s.shape,0)
        w=(s-c_ref[:,0:1])*jnp.where(row<6,s[6:7],1.0)
        p=[]
        for _ in range(3):
            h=w.astype(B).astype(F); p.append(h); w=w-h
        wt[...]=jnp.concatenate(p+[jnp.zeros((8,TS),F)],axis=0).astype(B)
        def chunk(k,_):
            cs=pl.ds(pl.multiple_of(k*CH,CH),CH)
            ww=jnp.concatenate([wt[:,cs],zw],axis=0)
            for mx in range(2): pltpu.matmul_push_rhs(ww,0,mx,transpose=True)
            st=[jnp.broadcast_to(st_ref[0,b,r:r+1,cs],(G,CH)) for r in range(6)]
            for g in range(NG):
                rs=slice(g*G,(g+1)*G)
                q=[jnp.concatenate([qb[c,rs,:]]*2,axis=1) for c in range(6)]
                dx,dy,dz,wx,wy,wz=[st[c]-q[c] for c in range(6)]
                s2=(dx*dx+dy*dy)+(dz*dz+0.01)
                dw=(dx*wx+dy*wy)+dz*wz
                r=lax.rsqrt(s2); r2=r*r; S=r2*r; T=S*(r2*dw)
                sh=S.astype(B); sl=(S-sh.astype(F)).astype(B)
                th=T.astype(B); tl=(T-th.astype(F)).astype(B)
                ld=0 if g==0 else None
                pltpu.matmul_acc_lhs(sacc[g],sh,load_staged_rhs=ld)
                pltpu.matmul_acc_lhs(tacc[g],th,load_staged_rhs=ld)
                pltpu.matmul_acc_lhs(sacc[g],sl)
                pltpu.matmul_acc_lhs(tacc[g],tl)
            return 0
        lax.fori_loop(0,TS//CH,chunk,0,unroll=4)
        return 0
    lax.fori_loop(0,BB,block,0)
    for g in range(NG):
        rs=slice(g*G,(g+1)*G)
        acc[0,rs,:]+=pltpu.matmul_pop(sacc[g])[:,:128]
        acc[1,rs,:]+=pltpu.matmul_pop(tacc[g])[:,:128]
    @pl.when(i==pl.num_programs(0)-1)
    def _():
        for c in range(2): o_ref[c]=acc[c].T[0:32]
def pair_sums(first, ranks, st, qc, c, G=16):
    R, BB, _, TS = st.shape
    pairs = A * ranks * BB * TS
    return pl.pallas_call(
        functools.partial(pair_kernel, G=G, BB=BB),
        grid_spec=pltpu.PrefetchScalarGridSpec(
            num_scalar_prefetch=1,
            grid=(ranks,),
            in_specs=[
                pl.BlockSpec((1, BB, 8, TS), lambda i, o: (lax.rem(i + o[0], R), 0, 0, 0)),
                pl.BlockSpec((A, 128), lambda i, o: (0, 0)),
                pl.BlockSpec((8, 128), lambda i, o: (0, 0)),
            ],
            out_specs=pl.BlockSpec((2, 32, A), lambda i, o: (0, 0, 0)),
            scratch_shapes=[
                pltpu.VMEM((6, A, 128), F),
                pltpu.VMEM((32, TS), B),
                pltpu.VMEM((2, A, 128), F),
            ],
        ),
        out_shape=jax.ShapeDtypeStruct((2, 32, A), F),
        compiler_params=pltpu.CompilerParams(vmem_limit_bytes=40 << 20),
        cost_estimate=pl.CostEstimate(
            flops=40 * pairs, bytes_accessed=32 * ranks * BB * TS, transcendentals=pairs
        ),
    )(first, st, qc, c)


def final_kernel(
    as_ref, st_ref, nb_ref, qc_ref, q_ref, c_ref, *rest
):
    *sums, start_ref, old_ref, h_ref, cor_ref, for_ref, near = rest

    def lanes(dev, g):
        row, col = lax.div(dev, st_ref.shape[1]), lax.rem(dev, st_ref.shape[1])
        return st_ref[row, col, :, g * 128 : (g + 1) * 128]

    def gather(t, _):
        a = t * 4
        for u in range(4):
            dev = as_ref[a + u]
            idx = jnp.broadcast_to(nb_ref[pl.ds(a + u, 1), :], (8, 128))
            near[a + u] = pick_columns(functools.partial(lanes, dev), idx & 127, idx >> 7)
        return 0

    lax.fori_loop(0, A // 4, gather, 0)
    d = [near[:, r, :] - qc_ref[:, r : r + 1] for r in range(6)]
    dx, dy, dz, wx, wy, wz = d
    dist = dx * dx + dy * dy + dz * dz + SOFT
    inv = 1.0 / dist
    strength = near[:, 6, :] * inv * jnp.sqrt(inv)
    radial = 3.0 * (dx * wx + dy * wy + dz * wz) * inv
    cols = [
        jnp.sum(x, axis=1, keepdims=True)
        for x in (
            strength * dx,
            strength * dy,
            strength * dz,
            strength * (wx - radial * dx),
            strength * (wy - radial * dy),
            strength * (wz - radial * dz),
        )
    ]
    irregular = jnp.concatenate(cols + [jnp.zeros((A, 122), F)], axis=1).T[0:6]
    p = sum(ref[...] for ref in sums[1:]) + sums[0][...]
    p = (p[:, 16:24] + p[:, 8:16]) + p[:, 0:8]
    q = q_ref[...] - c_ref[:, 0:1]
    ps, pt = p[0], p[1]
    acc = ps[0:3] - q[0:3] * ps[6:7]
    jerk = (ps[3:6] - q[3:6] * ps[6:7]) - 3.0 * (pt[0:3] - q[0:3] * pt[6:7])
    total = jnp.concatenate([acc, jerk])
    for_ref[...] = jnp.concatenate([total - irregular, irregular])
    h = h_ref[...]
    half = h * 0.5
    twelfth = h * h / 12.0
    a0, j0 = old_ref[0:3, :], old_ref[3:6, :]
    x0, v0 = start_ref[0:3, :], start_ref[3:6, :]
    v1 = v0 + (a0 + acc) * half + (j0 - jerk) * twelfth
    x1 = x0 + (v0 + v1) * half + (a0 - acc) * twelfth
    cor_ref[...] = jnp.concatenate([x1, v1])


def finish(assignment, st, neighbours, qc, q, c, sums, start, old, step):
    whole = pl.BlockSpec(memory_space=pltpu.VMEM)
    return pl.pallas_call(
        final_kernel,
        in_specs=[pl.BlockSpec(memory_space=pltpu.SMEM)] + [whole] * (8 + len(sums)),
        out_specs=(whole, whole),
        out_shape=(jax.ShapeDtypeStruct((6, A), F), jax.ShapeDtypeStruct((12, A), F)),
        scratch_shapes=[pltpu.VMEM((A, 8, 128), F)],
        compiler_params=pltpu.CompilerParams(vmem_limit_bytes=40 << 20),
    )(assignment[:, 0], st, neighbours, qc, q, c, *sums, start, old, step[None, :])


def body(star_state, active_index, neighbour_index, assignment, start_state, old_derivs, step_size):
    rows = lax.axis_size("row")
    stars = jnp.pad(star_state, ((0, 1), (0, 0)))
    group = lax.all_gather(stars, "col")
    ahead = [
        lax.ppermute(group, "row", [((r + step) % rows, r) for r in range(rows)]) for step in range(1, AHEAD + 1)
    ]
    every = lax.all_gather(group, "row")
    q, qc, c = own_states(stars, active_index)
    zero = jnp.zeros((1,), jnp.int32)
    after = (lax.axis_index("row") + 1 + AHEAD).astype(jnp.int32).reshape(1)
    sums = [pair_sums(zero, 1, g[None], qc, c) for g in [group, *ahead]]
    sums.append(pair_sums(after, rows - 1 - AHEAD, every, qc, c))
    return finish(assignment, every, neighbour_index, qc, q, c, sums, start_state, old_derivs, step_size)


def solution(mesh):
    both = ("row", "col")
    in_specs = (P(None, both), P(both), P(both, None), P(both, None), P(None, both), P(None, both), P(both))
    out_specs = (P(None, both), P(None, both))
    return jax.shard_map(body, mesh=mesh, in_specs=in_specs, out_specs=out_specs, check_vma=False)
```

```python
import functools

import jax
import jax.numpy as jnp
from jax import lax
from jax.experimental import pallas as pl
from jax.experimental.pallas import tpu as pltpu
from jax.sharding import PartitionSpec as P

F = jnp.float32
B = jnp.bfloat16
SOFT = 0.01
A = 256
K = 128
S = 2048
CH = 256
SIDE = 4
AHEAD = (1, 3, 4, 12, 2)


def pick_columns(table, low, high):
    out = jnp.zeros(low.shape, F)
    for g in range(S // 128):
        found = jnp.take_along_axis(table(g), low, axis=1, mode="promise_in_bounds")
        out = jnp.where(high == g, found, out)
    return out


def own_kernel(st_ref, idx_ref, q_ref, qc_ref, c_ref):
    for h in range(A // 128):
        idx = jnp.broadcast_to(idx_ref[0:1, h * 128 : (h + 1) * 128], (8, 128))
        table = lambda g: st_ref[:, g * 128 : (g + 1) * 128]
        q_ref[:, h * 128 : (h + 1) * 128] = pick_columns(table, idx & 127, idx >> 7)
    q = q_ref[...]
    row = lax.broadcasted_iota(jnp.int32, q.shape, 0)
    q = jnp.where(row < 6, q, 0.0)
    q_ref[...] = q
    wide = jnp.concatenate([q, jnp.zeros((120, A), F)])
    qc_ref[...] = wide.T
    c_ref[...] = jnp.broadcast_to(jnp.sum(q, axis=1, keepdims=True) * (1.0 / A), (8, 128))


def own_states(stars, active_index):
    return pl.pallas_call(
        own_kernel,
        out_shape=(
            jax.ShapeDtypeStruct((8, A), F),
            jax.ShapeDtypeStruct((A, 128), F),
            jax.ShapeDtypeStruct((8, 128), F),
        ),
    )(stars, active_index[None, :])


def pair_kernel(*refs, G, BB):
    NG=A//G
    pl.run_scoped(functools.partial(pair_body,*refs,G=G,BB=BB),*([pltpu.ACC(0)((G,256),F)]*NG+[pltpu.ACC(1)((G,256),F)]*NG))
def pair_body(_, st_ref, qc_ref, c_ref, o_ref, qb, wt, acc, *accs, G, BB):
    NG=A//G
    sacc=accs[:NG]; tacc=accs[NG:]
    TS=st_ref.shape[3]
    i=pl.program_id(0)
    @pl.when(i==0)
    def _():
        for c in range(6):
            qb[c]=jnp.broadcast_to(qc_ref[:,c:c+1],(A,128))
        acc[...]=jnp.zeros_like(acc)
    zw=jnp.zeros((256-32,CH),B)
    def block(b, _):
        s=st_ref[0,b]
        row=lax.broadcasted_iota(jnp.int32,s.shape,0)
        w=(s-c_ref[:,0:1])*jnp.where(row<6,s[6:7],1.0)
        p=[]
        for _ in range(3):
            h=w.astype(B).astype(F); p.append(h); w=w-h
        wt[...]=jnp.concatenate(p+[jnp.zeros((8,TS),F)],axis=0).astype(B)
        def chunk(k,_):
            cs=pl.ds(pl.multiple_of(k*CH,CH),CH)
            ww=jnp.concatenate([wt[:,cs],zw],axis=0)
            for mx in range(2): pltpu.matmul_push_rhs(ww,0,mx,transpose=True)
            st=[jnp.broadcast_to(st_ref[0,b,r:r+1,cs],(G,CH)) for r in range(6)]
            for g in range(NG):
                rs=slice(g*G,(g+1)*G)
                q=[jnp.concatenate([qb[c,rs,:]]*2,axis=1) for c in range(6)]
                dx,dy,dz,wx,wy,wz=[st[c]-q[c] for c in range(6)]
                s2=(dx*dx+dy*dy)+(dz*dz+0.01)
                dw=(dx*wx+dy*wy)+dz*wz
                r=lax.rsqrt(s2); r2=r*r; S=r2*r; T=S*(r2*dw)
                sh=S.astype(B); sl=(S-sh.astype(F)).astype(B)
                th=T.astype(B); tl=(T-th.astype(F)).astype(B)
                ld=0 if g==0 else None
                pltpu.matmul_acc_lhs(sacc[g],sh,load_staged_rhs=ld)
                pltpu.matmul_acc_lhs(tacc[g],th,load_staged_rhs=ld)
                pltpu.matmul_acc_lhs(sacc[g],sl)
                pltpu.matmul_acc_lhs(tacc[g],tl)
            return 0
        lax.fori_loop(0,TS//CH,chunk,0,unroll=4)
        return 0
    lax.fori_loop(0,BB,block,0)
    for g in range(NG):
        rs=slice(g*G,(g+1)*G)
        acc[0,rs,:]+=pltpu.matmul_pop(sacc[g])[:,:128]
        acc[1,rs,:]+=pltpu.matmul_pop(tacc[g])[:,:128]
    @pl.when(i==pl.num_programs(0)-1)
    def _():
        for c in range(2): o_ref[c]=acc[c].T[0:32]
def pair_sums(order, st, qc, c, G=16):
    _, BB, _, TS = st.shape
    ranks = order.shape[0]
    pairs = A * ranks * BB * TS
    return pl.pallas_call(
        functools.partial(pair_kernel, G=G, BB=BB),
        grid_spec=pltpu.PrefetchScalarGridSpec(
            num_scalar_prefetch=1,
            grid=(ranks,),
            in_specs=[
                pl.BlockSpec((1, BB, 8, TS), lambda i, o: (o[i], 0, 0, 0)),
                pl.BlockSpec((A, 128), lambda i, o: (0, 0)),
                pl.BlockSpec((8, 128), lambda i, o: (0, 0)),
            ],
            out_specs=pl.BlockSpec((2, 32, A), lambda i, o: (0, 0, 0)),
            scratch_shapes=[
                pltpu.VMEM((6, A, 128), F),
                pltpu.VMEM((32, TS), B),
                pltpu.VMEM((2, A, 128), F),
            ],
        ),
        out_shape=jax.ShapeDtypeStruct((2, 32, A), F),
        compiler_params=pltpu.CompilerParams(vmem_limit_bytes=40 << 20),
        cost_estimate=pl.CostEstimate(
            flops=40 * pairs, bytes_accessed=32 * ranks * BB * TS, transcendentals=pairs
        ),
    )(order, st, qc, c)


def final_kernel(
    as_ref, st_ref, nb_ref, qc_ref, q_ref, c_ref, *rest
):
    *sums, start_ref, old_ref, h_ref, cor_ref, for_ref, near = rest

    def lanes(dev, g):
        row, col = lax.div(dev, st_ref.shape[1]), lax.rem(dev, st_ref.shape[1])
        return st_ref[row, col, :, g * 128 : (g + 1) * 128]

    def gather(t, _):
        a = t * 4
        for u in range(4):
            dev = as_ref[a + u]
            idx = jnp.broadcast_to(nb_ref[pl.ds(a + u, 1), :], (8, 128))
            near[a + u] = pick_columns(functools.partial(lanes, dev), idx & 127, idx >> 7)
        return 0

    lax.fori_loop(0, A // 4, gather, 0)
    d = [near[:, r, :] - qc_ref[:, r : r + 1] for r in range(6)]
    dx, dy, dz, wx, wy, wz = d
    dist = dx * dx + dy * dy + dz * dz + SOFT
    inv = 1.0 / dist
    strength = near[:, 6, :] * inv * jnp.sqrt(inv)
    radial = 3.0 * (dx * wx + dy * wy + dz * wz) * inv
    cols = [
        jnp.sum(x, axis=1, keepdims=True)
        for x in (
            strength * dx,
            strength * dy,
            strength * dz,
            strength * (wx - radial * dx),
            strength * (wy - radial * dy),
            strength * (wz - radial * dz),
        )
    ]
    irregular = jnp.concatenate(cols + [jnp.zeros((A, 122), F)], axis=1).T[0:6]
    p = sum(ref[...] for ref in sums[1:]) + sums[0][...]
    p = (p[:, 16:24] + p[:, 8:16]) + p[:, 0:8]
    q = q_ref[...] - c_ref[:, 0:1]
    ps, pt = p[0], p[1]
    acc = ps[0:3] - q[0:3] * ps[6:7]
    jerk = (ps[3:6] - q[3:6] * ps[6:7]) - 3.0 * (pt[0:3] - q[0:3] * pt[6:7])
    total = jnp.concatenate([acc, jerk])
    for_ref[...] = jnp.concatenate([total - irregular, irregular])
    h = h_ref[...]
    half = h * 0.5
    twelfth = h * h / 12.0
    a0, j0 = old_ref[0:3, :], old_ref[3:6, :]
    x0, v0 = start_ref[0:3, :], start_ref[3:6, :]
    v1 = v0 + (a0 + acc) * half + (j0 - jerk) * twelfth
    x1 = x0 + (v0 + v1) * half + (a0 - acc) * twelfth
    cor_ref[...] = jnp.concatenate([x1, v1])


def finish(assignment, st, neighbours, qc, q, c, sums, start, old, step):
    whole = pl.BlockSpec(memory_space=pltpu.VMEM)
    return pl.pallas_call(
        final_kernel,
        in_specs=[pl.BlockSpec(memory_space=pltpu.SMEM)] + [whole] * (8 + len(sums)),
        out_specs=(whole, whole),
        out_shape=(jax.ShapeDtypeStruct((6, A), F), jax.ShapeDtypeStruct((12, A), F)),
        scratch_shapes=[pltpu.VMEM((A, 8, 128), F)],
        compiler_params=pltpu.CompilerParams(vmem_limit_bytes=40 << 20),
    )(assignment[:, 0], st, neighbours, qc, q, c, *sums, start, old, step[None, :])


def neighbour(row, step):
    z = (row % SIDE + step % SIDE) % SIDE
    y = (row // SIDE + step // SIDE) % SIDE
    return y * SIDE + z


def body(star_state, active_index, neighbour_index, assignment, start_state, old_derivs, step_size):
    rows = lax.axis_size("row")
    stars = jnp.pad(star_state, ((0, 1), (0, 0)))
    group = lax.all_gather(stars, "col")
    ahead = [lax.ppermute(group, "row", [(neighbour(r, s), r) for r in range(rows)]) for s in AHEAD]
    every = lax.all_gather(group, "row")
    q, qc, c = own_states(stars, active_index)
    zero = jnp.zeros((1,), jnp.int32)
    rest = [s for s in range(1, rows) if s not in AHEAD]
    me = lax.axis_index("row")
    order = jnp.stack([neighbour(me, s) for s in rest]).astype(jnp.int32)
    sums = [pair_sums(zero, g[None], qc, c) for g in [group, *ahead]]
    sums.append(pair_sums(order, every, qc, c))
    return finish(assignment, every, neighbour_index, qc, q, c, sums, start_state, old_derivs, step_size)


def solution(mesh):
    both = ("row", "col")
    in_specs = (P(None, both), P(both), P(both, None), P(both, None), P(None, both), P(None, both), P(both))
    out_specs = (P(None, both), P(None, both))
    return jax.shard_map(body, mesh=mesh, in_specs=in_specs, out_specs=out_specs, check_vma=False)
```
